32 devices in a mesh: row: 8 (over y, x, core), col: 4 (over z).
Axes of the slice: x: 2, y: 2, z: 4, core: 2. Of those that a mesh axis runs over, the one named last changes fastest.
Arguments:
- left_factor: bfloat16 [2, 512, 2048], P(None, 'col', 'row'), may hold values from -6 to 6
- right_factor: bfloat16 [2, 512, 1024], P(None, 'row', 'col'), may hold values from -0.1875 to 0.1875
- recorded: bfloat16 [2, 2048, 1024], P(None, 'row', 'col'), may hold values from -6 to 6
- partner: int32 [1024], replicated, may hold values from 0 to 1023, as said below
- delay: int32 [1024], replicated, may hold values from 0 to 63
Outputs:
- left_out: bfloat16 [2, 512, 2048], P(None, 'col', 'row')
- right_out: bfloat16 [2, 512, 1024], P(None, 'row', 'col')
The draws below stay inside these ranges and needn't reach their ends.
Inputs may be any that keep to these rules, and one draw needn't show every extreme that they name: partner[s] lies in the block of 256 consecutive shots that holds s (blocks start at multiples of 256) or in the block after it, the last block being followed by the first; a shot may be its own partner, and some shots are the partner of many shots.
All inputs are finite; a program needn't handle non-finite values.
Results may differ from the reference program's by a relative error of at most 0.011.
Values may be sent and summed in bfloat16 or wider, within the bound.
No kernel may reach another device: no remote copies, remote signals or barrier semaphores. Data moves between devices by JAX's collectives and lax.ppermute only.
A program may use at most 64 MiB of HBM per device.

```python
import math
import jax
import jax.numpy as jnp

RANK = 512
COL_DEV = 256
ITERS = 2
NDELAY = 64
NR = 2048
NC = 1024


def draw_partner(key, part):
    width = 2 * COL_DEV
    picks = jax.random.randint(jax.random.fold_in(key, 17), (NC,), 0, width)
    offset = picks * picks // width
    shots = jnp.arange(NC, dtype=jnp.int32)
    base = shots // COL_DEV * COL_DEV
    return jnp.mod(base + offset, NC).astype(jnp.int32)


def set_ends(values, own_key, low, high):
    place = [jax.random.randint(jax.random.fold_in(own_key, axis), (), 0, length) for axis, length in enumerate(values.shape)]
    longest = values.shape.index(max(values.shape))
    beside = place[:longest] + [(place[longest] + 1) % values.shape[longest]] + place[longest + 1:]
    return values.at[tuple(place)].set(low).at[tuple(beside)].set(high)


def steps_of(own_key, dims, split, least, top_value):
    gain, own = 1.0, jax.random.fold_in(own_key, 6)
    for dim, parts in split:
        heights = jnp.exp(jax.random.uniform(jax.random.fold_in(own, dim), (parts,), jnp.float32, least / len(split), top_value / len(split)))
        gain = gain * jnp.repeat(heights, dims[dim] // parts).reshape([-1 if axis == dim else 1 for axis in range(len(dims))])
    return gain


def centred(stream_key, dims, spread, limit, split=(), kind=jnp.bfloat16):
    drawn = jax.random.normal(stream_key, dims, jnp.float32) * spread
    if len(split) > 0:
        drawn = steps_of(stream_key, dims, split, -0.22, 0.18) * drawn
    return jnp.clip(drawn, min=-limit, max=limit).astype(kind)


def setup_inputs(seed: int = 0) -> dict:
    key_of = jax.random.split(jax.random.key(seed), 6)
    return {
        "left_factor": centred(key_of[0], (2, RANK, NR), 1.0, 6.0, ((1, 4), (2, 8))),
        "right_factor": centred(key_of[1], (2, RANK, NC), (2 * RANK) ** -0.5, 0.1875, ((1, 8), (2, 4))),
        "recorded": centred(key_of[2], (2, NR, NC), 1.0, 6.0, ((1, 8), (2, 4))),
        "partner": draw_partner(jax.random.fold_in(key_of[5], 71), 0),
        "delay": set_ends(jax.random.randint(key_of[4], (NC,), 0, NDELAY), jax.random.fold_in(key_of[4], 1), 0, NDELAY - 1).astype(jnp.int32),
    }


def reference(left_factor, right_factor, recorded, partner, delay):
    theta = 2.0 * math.pi * delay.astype(jnp.float32) / NDELAY
    pcos = jnp.cos(theta)
    psin = jnp.sin(theta)
    qcos = pcos[partner]
    qsin = psin[partner]
    eta_left = 0.1 * math.sqrt(RANK / NC)
    eta_right = 0.05 / math.sqrt(RANK * NR)
    rec = recorded.astype(jnp.float32)
    lft = left_factor
    rgt = right_factor
    for step in range(ITERS):
        lr = lft[0].astype(jnp.float32)
        li = lft[1].astype(jnp.float32)
        rr = rgt[0].astype(jnp.float32)
        ri = rgt[1].astype(jnp.float32)
        xr = jnp.einsum('kr,kc->rc', lr, rr) + jnp.einsum('kr,kc->rc', li, ri)
        xi = jnp.einsum('kr,kc->rc', li, rr) - jnp.einsum('kr,kc->rc', lr, ri)
        xr = xr.astype(jnp.bfloat16).astype(jnp.float32)
        xi = xi.astype(jnp.bfloat16).astype(jnp.float32)
        yr = jnp.take(xr, partner, axis=1)
        yi = jnp.take(xi, partner, axis=1)
        br = pcos * xr - psin * xi + qcos * yr - qsin * yi - rec[0]
        bi = pcos * xi + psin * xr + qcos * yi + qsin * yr - rec[1]
        br = br.astype(jnp.bfloat16).astype(jnp.float32)
        bi = bi.astype(jnp.bfloat16).astype(jnp.float32)
        extra_r = jax.ops.segment_sum(br.T, partner, num_segments=NC).T
        extra_i = jax.ops.segment_sum(bi.T, partner, num_segments=NC).T
        ar = br + extra_r
        ai = bi + extra_i
        gr = (pcos * ar + psin * ai).astype(jnp.bfloat16).astype(jnp.float32)
        gi = (pcos * ai - psin * ar).astype(jnp.bfloat16).astype(jnp.float32)
        glr = jnp.einsum('kc,rc->kr', rr, gr) - jnp.einsum('kc,rc->kr', ri, gi)
        gli = jnp.einsum('kc,rc->kr', ri, gr) + jnp.einsum('kc,rc->kr', rr, gi)
        grr = jnp.einsum('kr,rc->kc', lr, gr) + jnp.einsum('kr,rc->kc', li, gi)
        gri = jnp.einsum('kr,rc->kc', li, gr) - jnp.einsum('kr,rc->kc', lr, gi)
        grad_left = jnp.stack([glr, gli])
        grad_right = jnp.stack([grr, gri])
        lft = (lft.astype(jnp.float32) - eta_left * grad_left).astype(jnp.bfloat16)
        rgt = (rgt.astype(jnp.float32) - eta_right * grad_right).astype(jnp.bfloat16)
    return (lft, rgt)
```

```python
import math

import jax
import jax.numpy as jnp
from jax import lax
from jax.sharding import PartitionSpec as P

ITERS = 2
NDELAY = 64
BF = jnp.bfloat16
F32 = jnp.float32


def exchanged(shard, axis, flip):
    size = lax.axis_size(axis)
    return lax.ppermute(shard, axis, [(i, i ^ flip) for i in range(size)])


def passed_along(shard, axis, by):
    size = lax.axis_size(axis)
    return lax.ppermute(shard, axis, [(i, (i + by) % size) for i in range(size)])


def in_order(parts, me, axis):
    stacked = jnp.stack(parts)
    order = jnp.bitwise_xor(lax.iota(jnp.int32, len(parts)), me)
    out = [lax.dynamic_index_in_dim(stacked, order[i], 0, False) for i in range(len(parts))]
    return jnp.concatenate(out, axis=1)


def gathered(shard, axis):
    size = lax.axis_size(axis)
    parts = [shard] + [exchanged(shard, axis, d) for d in range(1, size)]
    return in_order(parts, lax.axis_index(axis), axis)


def scattered_sum(whole, axis):
    size = lax.axis_size(axis)
    me = lax.axis_index(axis)
    width = whole.shape[1] // size
    total = lax.dynamic_slice_in_dim(whole, me * width, width, 1)
    for d in range(1, size):
        part = lax.dynamic_slice_in_dim(whole, (me ^ d) * width, width, 1).astype(BF)
        total = total + exchanged(part, axis, d).astype(F32)
    return total


def mult(spec, a, b):
    return jnp.einsum(spec, a, b, preferred_element_type=F32)


def on_device(left_factor, right_factor, recorded, partner, delay):
    shots_dev = recorded.shape[2]
    rows_dev = recorded.shape[1]
    shots_all = partner.shape[0]
    rows_all = rows_dev * lax.axis_size("row")
    rank_full = left_factor.shape[1] * lax.axis_size("col")
    eta_left = 0.1 * math.sqrt(rank_full / shots_all)
    eta_right = 0.05 / math.sqrt(rank_full * rows_all)
    block = lax.axis_index("col")
    blocks = lax.axis_size("col")

    def of_block(vector, by):
        return lax.dynamic_slice_in_dim(vector, jnp.mod(block + by, blocks) * shots_dev, shots_dev, 0)

    def picks(by):
        start = jnp.mod(block + by, blocks) * shots_dev
        near = jnp.mod(of_block(partner, by) - start, shots_all)
        return (lax.broadcasted_iota(jnp.int32, (2 * shots_dev, shots_dev), 0) == near[None, :]).astype(BF)

    def phases(values):
        theta = 2.0 * math.pi * values / NDELAY
        return jnp.cos(theta), jnp.sin(theta)

    pick_prev, pick_own, pick_next = picks(-1), picks(0), picks(1)
    delay_own, delay_next = of_block(delay, 0).astype(F32), of_block(delay, 1).astype(F32)
    both = jnp.concatenate([delay_own, delay_next]).astype(BF)
    delay_part = mult("c,cs->s", both, pick_own)
    cos_own, sin_own = phases(delay_own)
    cos_next, sin_next = phases(delay_next)
    cos_part, sin_part = phases(delay_part)

    def mixed(right_own, right_next):
        pair = jnp.concatenate([right_own, right_next], axis=2)
        part = mult("zkc,cs->zks", pair, pick_own)
        own = right_own.astype(F32)
        real = cos_own * own[0] + sin_own * own[1] + cos_part * part[0] + sin_part * part[1]
        imag = cos_own * own[1] - sin_own * own[0] + cos_part * part[1] - sin_part * part[0]
        return jnp.stack([real, imag]).astype(BF)

    def folded(w_prev, w_own, pick_before, pick_here, cos, sin):
        s = w_own.astype(F32)
        s = s + mult("zks,cs->zkc", w_prev, pick_before[shots_dev:]) + mult("zks,cs->zkc", w_own, pick_here[:shots_dev])
        return jnp.stack([cos * s[0] - sin * s[1], cos * s[1] + sin * s[0]])

    rec = recorded.astype(F32)
    left = left_factor
    right = right_factor
    right_next = passed_along(right, "col", -1)
    for step in range(ITERS):
        mixed_shard = mixed(right, right_next)
        q = gathered(mixed_shard, "row")
        lw = gathered(left, "col")
        br = mult("kr,kc->rc", lw[0], q[0]) + mult("kr,kc->rc", lw[1], q[1]) - rec[0]
        bi = mult("kr,kc->rc", lw[1], q[0]) - mult("kr,kc->rc", lw[0], q[1]) - rec[1]
        br, bi = br.astype(BF), bi.astype(BF)
        wr = mult("kr,rc->kc", lw[0], br) + mult("kr,rc->kc", lw[1], bi)
        wi = mult("kr,rc->kc", lw[1], br) - mult("kr,rc->kc", lw[0], bi)
        glr = mult("kc,rc->kr", q[0], br) - mult("kc,rc->kr", q[1], bi)
        gli = mult("kc,rc->kr", q[1], br) + mult("kc,rc->kr", q[0], bi)
        w_own = scattered_sum(jnp.stack([wr, wi]), "row").astype(BF)
        w_prev = passed_along(w_own, "col", 1)
        left = (left.astype(F32) - eta_left * scattered_sum(jnp.stack([glr, gli]), "col")).astype(BF)
        if step + 1 < ITERS:
            w_next = passed_along(w_own, "col", -1)
            grad_next = folded(w_own, w_next, pick_own, pick_next, cos_next, sin_next)
            right_next = (right_next.astype(F32) - eta_right * grad_next).astype(BF)
        grad_own = folded(w_prev, w_own, pick_prev, pick_own, cos_own, sin_own)
        right = (right.astype(F32) - eta_right * grad_own).astype(BF)
    return (left, right)


def solution(mesh):
    in_specs = (P(None, "col", "row"), P(None, "row", "col"), P(None, "row", "col"), P(), P())
    out_specs = (P(None, "col", "row"), P(None, "row", "col"))
    return jax.shard_map(
        on_device, mesh=mesh, in_specs=in_specs, out_specs=out_specs, check_vma=False
    )
```

```python
import math

import jax
import jax.numpy as jnp
from jax import lax
from jax.sharding import PartitionSpec as P

ITERS = 2
NDELAY = 64
BF = jnp.bfloat16
F32 = jnp.float32


def exchanged(shard, axis, flip):
    size = lax.axis_size(axis)
    return lax.ppermute(shard, axis, [(i, i ^ flip) for i in range(size)])


def passed_along(shard, axis, by):
    size = lax.axis_size(axis)
    return lax.ppermute(shard, axis, [(i, (i + by) % size) for i in range(size)])


def placed(parts, me):
    width = parts[0].shape[1]
    whole = jnp.zeros(
        (parts[0].shape[0], width * len(parts)) + parts[0].shape[2:], parts[0].dtype
    )
    for d, part in enumerate(parts):
        whole = lax.dynamic_update_slice_in_dim(whole, part, (me ^ d) * width, 1)
    return whole


def gathered_left(shard):
    size = lax.axis_size("col")
    parts = [shard] + [exchanged(shard, "col", d) for d in range(1, size)]
    return placed(parts, lax.axis_index("col"))


def gathered_right(shard):
    size = lax.axis_size("row")
    me = lax.axis_index("row")
    same = shard[:, None]
    parts = [same] + [exchanged(same, "row", d) for d in range(2, size, 2)]
    half = placed(parts, me >> 1)
    other = exchanged(half, "row", 1)
    whole = jnp.zeros((half.shape[0], half.shape[1], 2) + half.shape[2:], half.dtype)
    whole = lax.dynamic_update_slice_in_dim(whole, half[:, :, None], me & 1, 2)
    whole = lax.dynamic_update_slice_in_dim(whole, other[:, :, None], (me & 1) ^ 1, 2)
    return whole.reshape(half.shape[0], -1, half.shape[3])


def scattered_left(whole):
    size = lax.axis_size("col")
    me = lax.axis_index("col")
    width = whole.shape[1] // size
    total = lax.dynamic_slice_in_dim(whole, me * width, width, 1)
    for d in range(1, size):
        part = lax.dynamic_slice_in_dim(whole, (me ^ d) * width, width, 1).astype(BF)
        total = total + exchanged(part, "col", d).astype(F32)
    return total


def scattered_right(whole):
    size = lax.axis_size("row")
    me = lax.axis_index("row")
    cut = whole.reshape(whole.shape[0], size // 2, 2, -1, whole.shape[2])
    mine = lax.dynamic_index_in_dim(cut, me & 1, 2, False)
    theirs = lax.dynamic_index_in_dim(cut, (me & 1) ^ 1, 2, False).astype(BF)
    pair = mine + exchanged(theirs, "row", 1).astype(F32)
    total = lax.dynamic_index_in_dim(pair, me >> 1, 1, False)
    for d in range(2, size, 2):
        part = lax.dynamic_index_in_dim(pair, (me ^ d) >> 1, 1, False).astype(BF)
        total = total + exchanged(part, "row", d).astype(F32)
    return total


def mult(spec, a, b):
    return jnp.einsum(spec, a, b, preferred_element_type=F32)


def on_device(left_factor, right_factor, recorded, partner, delay):
    shots_dev = recorded.shape[2]
    rows_dev = recorded.shape[1]
    shots_all = partner.shape[0]
    rows_all = rows_dev * lax.axis_size("row")
    rank_full = left_factor.shape[1] * lax.axis_size("col")
    eta_left = 0.1 * math.sqrt(rank_full / shots_all)
    eta_right = 0.05 / math.sqrt(rank_full * rows_all)
    block = lax.axis_index("col")
    blocks = lax.axis_size("col")

    def of_block(vector, by):
        return lax.dynamic_slice_in_dim(vector, jnp.mod(block + by, blocks) * shots_dev, shots_dev, 0)

    def picks(by):
        start = jnp.mod(block + by, blocks) * shots_dev
        near = jnp.mod(of_block(partner, by) - start, shots_all)
        return (lax.broadcasted_iota(jnp.int32, (2 * shots_dev, shots_dev), 0) == near[None, :]).astype(BF)

    def phases(values):
        theta = 2.0 * math.pi * values / NDELAY
        return jnp.cos(theta), jnp.sin(theta)

    pick_prev, pick_own, pick_next = picks(-1), picks(0), picks(1)
    delay_own, delay_next = of_block(delay, 0).astype(F32), of_block(delay, 1).astype(F32)
    both = jnp.concatenate([delay_own, delay_next]).astype(BF)
    delay_part = mult("c,cs->s", both, pick_own)
    cos_own, sin_own = phases(delay_own)
    cos_next, sin_next = phases(delay_next)
    cos_part, sin_part = phases(delay_part)

    def mixed(right_own, right_next):
        pair = jnp.concatenate([right_own, right_next], axis=2)
        part = mult("zkc,cs->zks", pair, pick_own)
        own = right_own.astype(F32)
        real = cos_own * own[0] + sin_own * own[1] + cos_part * part[0] + sin_part * part[1]
        imag = cos_own * own[1] - sin_own * own[0] + cos_part * part[1] - sin_part * part[0]
        return jnp.stack([real, imag]).astype(BF)

    def folded(w_prev, w_own, pick_before, pick_here, cos, sin):
        s = w_own.astype(F32)
        s = s + mult("zks,cs->zkc", w_prev, pick_before[shots_dev:]) + mult("zks,cs->zkc", w_own, pick_here[:shots_dev])
        return jnp.stack([cos * s[0] - sin * s[1], cos * s[1] + sin * s[0]])

    rec = recorded.astype(F32)
    left = left_factor
    right = right_factor
    right_next = passed_along(right, "col", -1)
    for step in range(ITERS):
        mixed_shard = mixed(right, right_next)
        q = gathered_right(mixed_shard)
        lw = gathered_left(left)
        br = mult("kr,kc->rc", lw[0], q[0]) + mult("kr,kc->rc", lw[1], q[1]) - rec[0]
        bi = mult("kr,kc->rc", lw[1], q[0]) - mult("kr,kc->rc", lw[0], q[1]) - rec[1]
        br, bi = br.astype(BF), bi.astype(BF)
        wr = mult("kr,rc->kc", lw[0], br) + mult("kr,rc->kc", lw[1], bi)
        wi = mult("kr,rc->kc", lw[1], br) - mult("kr,rc->kc", lw[0], bi)
        glr = mult("kc,rc->kr", q[0], br) - mult("kc,rc->kr", q[1], bi)
        gli = mult("kc,rc->kr", q[1], br) + mult("kc,rc->kr", q[0], bi)
        w_own = scattered_right(jnp.stack([wr, wi])).astype(BF)
        w_prev = passed_along(w_own, "col", 1)
        left = (left.astype(F32) - eta_left * scattered_left(jnp.stack([glr, gli]))).astype(BF)
        if step + 1 < ITERS:
            w_next = passed_along(w_own, "col", -1)
            grad_next = folded(w_own, w_next, pick_own, pick_next, cos_next, sin_next)
            right_next = (right_next.astype(F32) - eta_right * grad_next).astype(BF)
        grad_own = folded(w_prev, w_own, pick_prev, pick_own, cos_own, sin_own)
        right = (right.astype(F32) - eta_right * grad_own).astype(BF)
    return (left, right)


def solution(mesh):
    in_specs = (P(None, "col", "row"), P(None, "row", "col"), P(None, "row", "col"), P(), P())
    out_specs = (P(None, "col", "row"), P(None, "row", "col"))
    return jax.shard_map(
        on_device, mesh=mesh, in_specs=in_specs, out_specs=out_specs, check_vma=False
    )
```

```python
import math

import jax
import jax.numpy as jnp
from jax import lax
from jax.sharding import PartitionSpec as P

ITERS = 2
NDELAY = 64
BF = jnp.bfloat16
F32 = jnp.float32


def exchanged(shard, axis, flip):
    size = lax.axis_size(axis)
    return lax.ppermute(shard, axis, [(i, i ^ flip) for i in range(size)])


def passed_along(shard, axis, by):
    size = lax.axis_size(axis)
    return lax.ppermute(shard, axis, [(i, (i + by) % size) for i in range(size)])


def placed(parts, me):
    width = parts[0].shape[1]
    whole = jnp.zeros(
        (parts[0].shape[0], width * len(parts)) + parts[0].shape[2:], parts[0].dtype
    )
    for d, part in enumerate(parts):
        whole = lax.dynamic_update_slice_in_dim(whole, part, (me ^ d) * width, 1)
    return whole


def gathered_left(shard, small):
    size = lax.axis_size("col")
    near = exchanged(shard, "col", 1)
    shard, small = lax.optimization_barrier((shard, small))
    parts = [shard, near] + [exchanged(shard, "col", d) for d in range(2, size)]
    return placed(parts, lax.axis_index("col")), small


def same_core():
    size = lax.axis_size("row")
    return [list(range(core, size, 2)) for core in range(2)]


def gathered_right(shard):
    core = lax.axis_index("row") & 1
    half = lax.all_gather(shard, "row", axis=1, axis_index_groups=same_core())
    other = exchanged(half, "row", 1)
    whole = jnp.zeros((half.shape[0], half.shape[1], 2) + half.shape[2:], half.dtype)
    whole = lax.dynamic_update_slice_in_dim(whole, half[:, :, None], core, 2)
    whole = lax.dynamic_update_slice_in_dim(whole, other[:, :, None], core ^ 1, 2)
    return whole.reshape(half.shape[0], -1, half.shape[3])


def scattered_left(whole):
    size = lax.axis_size("col")
    me = lax.axis_index("col")
    width = whole.shape[1] // size
    terms = [lax.dynamic_slice_in_dim(whole, me * width, width, 1)]
    for d in range(1, size):
        part = lax.dynamic_slice_in_dim(whole, (me ^ d) * width, width, 1).astype(BF)
        terms.append(exchanged(part, "col", d))
    return terms


def scattered_right(whole):
    size = lax.axis_size("row")
    core = lax.axis_index("row") & 1
    cut = whole.reshape(whole.shape[0], size // 2, 2, -1, whole.shape[2])
    mine = lax.dynamic_index_in_dim(cut, core, 2, False)
    theirs = lax.dynamic_index_in_dim(cut, core ^ 1, 2, False).astype(BF)
    pair = mine + exchanged(theirs, "row", 1).astype(F32)
    parts = jnp.moveaxis(pair, 1, 0).astype(BF)
    parts = lax.all_to_all(parts, "row", 0, 0, axis_index_groups=same_core())
    return jnp.sum(parts.astype(F32), axis=0)


def mult(spec, a, b):
    return jnp.einsum(spec, a, b, preferred_element_type=F32)


def on_device(left_factor, right_factor, recorded, partner, delay):
    shots_dev = recorded.shape[2]
    rows_dev = recorded.shape[1]
    shots_all = partner.shape[0]
    rows_all = rows_dev * lax.axis_size("row")
    rank_full = left_factor.shape[1] * lax.axis_size("col")
    eta_left = 0.1 * math.sqrt(rank_full / shots_all)
    eta_right = 0.05 / math.sqrt(rank_full * rows_all)
    block = lax.axis_index("col")
    blocks = lax.axis_size("col")

    def of_block(vector, by):
        return lax.dynamic_slice_in_dim(vector, jnp.mod(block + by, blocks) * shots_dev, shots_dev, 0)

    def picks(by):
        start = jnp.mod(block + by, blocks) * shots_dev
        near = jnp.mod(of_block(partner, by) - start, shots_all)
        return (lax.broadcasted_iota(jnp.int32, (2 * shots_dev, shots_dev), 0) == near[None, :]).astype(BF)

    def phases(values):
        theta = 2.0 * math.pi * values / NDELAY
        return jnp.cos(theta), jnp.sin(theta)

    pick_prev, pick_own, pick_next = picks(-1), picks(0), picks(1)
    delay_own, delay_next = of_block(delay, 0).astype(F32), of_block(delay, 1).astype(F32)
    both = jnp.concatenate([delay_own, delay_next]).astype(BF)
    delay_part = mult("c,cs->s", both, pick_own)
    cos_own, sin_own = phases(delay_own)
    cos_next, sin_next = phases(delay_next)
    cos_part, sin_part = phases(delay_part)

    def mixed(right_own, right_next):
        pair = jnp.concatenate([right_own, right_next], axis=2)
        part = mult("zkc,cs->zks", pair, pick_own)
        own = right_own.astype(F32)
        real = cos_own * own[0] + sin_own * own[1] + cos_part * part[0] + sin_part * part[1]
        imag = cos_own * own[1] - sin_own * own[0] + cos_part * part[1] - sin_part * part[0]
        return jnp.stack([real, imag]).astype(BF)

    def folded(w_prev, w_own, pick_before, pick_here, cos, sin):
        s = w_own.astype(F32)
        s = s + mult("zks,cs->zkc", w_prev, pick_before[shots_dev:]) + mult("zks,cs->zkc", w_own, pick_here[:shots_dev])
        return jnp.stack([cos * s[0] - sin * s[1], cos * s[1] + sin * s[0]])

    rec = recorded.astype(F32)
    left = left_factor
    right = right_factor
    right_next = passed_along(right, "col", -1)
    lw, right_next = gathered_left(left, right_next)
    for step in range(ITERS):
        mixed_shard = mixed(right, right_next)
        q = gathered_right(mixed_shard)
        br = mult("kr,kc->rc", lw[0], q[0]) + mult("kr,kc->rc", lw[1], q[1]) - rec[0]
        bi = mult("kr,kc->rc", lw[1], q[0]) - mult("kr,kc->rc", lw[0], q[1]) - rec[1]
        br, bi = br.astype(BF), bi.astype(BF)
        wr = mult("kr,rc->kc", lw[0], br) + mult("kr,rc->kc", lw[1], bi)
        wi = mult("kr,rc->kc", lw[1], br) - mult("kr,rc->kc", lw[0], bi)
        glr = mult("kc,rc->kr", q[0], br) - mult("kc,rc->kr", q[1], bi)
        gli = mult("kc,rc->kr", q[1], br) + mult("kc,rc->kr", q[0], bi)
        w_own = scattered_right(jnp.stack([wr, wi])).astype(BF)
        last = step + 1 == ITERS
        terms = scattered_left(jnp.stack([glr, gli]))
        terms, w_own = lax.optimization_barrier((terms, w_own))
        beside = [passed_along(w_own, "col", by) for by in ((1,) if last else (1, -1))]
        left = (left.astype(F32) - eta_left * sum(t.astype(F32) for t in terms)).astype(BF)
        if last:
            left, beside = lax.optimization_barrier((left, beside))
        else:
            lw, beside = gathered_left(left, beside)
            grad_next = folded(w_own, beside[1], pick_own, pick_next, cos_next, sin_next)
            right_next = (right_next.astype(F32) - eta_right * grad_next).astype(BF)
        grad_own = folded(beside[0], w_own, pick_prev, pick_own, cos_own, sin_own)
        right = (right.astype(F32) - eta_right * grad_own).astype(BF)
    return (left, right)


def solution(mesh):
    in_specs = (P(None, "col", "row"), P(None, "row", "col"), P(None, "row", "col"), P(), P())
    out_specs = (P(None, "col", "row"), P(None, "row", "col"))
    return jax.shard_map(
        on_device, mesh=mesh, in_specs=in_specs, out_specs=out_specs, check_vma=False
    )
```

```python
import functools
import math

import jax
import jax.numpy as jnp
from jax import lax
from jax.experimental import pallas as pl
from jax.experimental.pallas import tpu as pltpu
from jax.sharding import PartitionSpec as P

ITERS = 2
NDELAY = 64
BF = jnp.bfloat16
F32 = jnp.float32


def exchanged(shard, axis, flip):
    size = lax.axis_size(axis)
    return lax.ppermute(shard, axis, [(i, i ^ flip) for i in range(size)])


def passed_along(shard, axis, by):
    size = lax.axis_size(axis)
    return lax.ppermute(shard, axis, [(i, (i + by) % size) for i in range(size)])


def same_core():
    size = lax.axis_size("row")
    return [list(range(core, size, 2)) for core in range(2)]


def gathered_left(shard, small, near_waits):
    size = lax.axis_size("col")
    held, small = lax.optimization_barrier((shard, small))
    parts = [shard]
    for d in range(1, size):
        parts.append(exchanged(held if (d == 1) == near_waits else shard, "col", d))
    return parts, small


def on_chip(kernel, outs, scratch=(), cost=1 << 20):
    return pl.pallas_call(
        kernel,
        out_shape=outs,
        scratch_shapes=list(scratch),
        cost_estimate=pl.CostEstimate(flops=cost, bytes_accessed=1 << 20, transcendentals=0),
        compiler_params=pltpu.CompilerParams(vmem_limit_bytes=48 * 1024 * 1024),
    )


def dot(a, b, ca, cb):
    return lax.dot_general(a, b, (((ca,), (cb,)), ((), ())), preferred_element_type=F32)


def stage_kernel(cols, *refs):
    left_refs, refs = refs[:cols], refs[cols:]
    q_own, q_other, rec, theirs, mine, *refs = refs
    left_outs, (lbuf, qbuf, wbuf, gbuf) = refs[:cols], refs[cols:]
    me, core = lax.axis_index("col"), lax.axis_index("row") & 1
    wide, narrow, chips = left_refs[0].shape[1], q_own.shape[2], q_own.shape[0]

    def left_rows(d):
        return pl.ds(pl.multiple_of((me ^ d) * wide, wide), wide)

    def right_rows(chip, which):
        return pl.ds(pl.multiple_of((2 * chip + which) * narrow, narrow), narrow)

    for d in range(cols):
        lbuf[:, left_rows(d), :] = left_refs[d][...]
    for chip in range(chips):
        qbuf[:, right_rows(chip, core), :] = q_own[chip]
        qbuf[:, right_rows(chip, core ^ 1), :] = q_other[chip]
    br = dot(lbuf[0], qbuf[0], 0, 0) + dot(lbuf[1], qbuf[1], 0, 0) - rec[0].astype(F32)
    bi = dot(lbuf[1], qbuf[0], 0, 0) - dot(lbuf[0], qbuf[1], 0, 0) - rec[1].astype(F32)
    br, bi = br.astype(BF), bi.astype(BF)
    wbuf[0] = dot(lbuf[0], br, 1, 0) + dot(lbuf[1], bi, 1, 0)
    wbuf[1] = dot(lbuf[1], br, 1, 0) - dot(lbuf[0], bi, 1, 0)
    for chip in range(chips):
        theirs[chip] = wbuf[:, right_rows(chip, core ^ 1), :].astype(BF)
        mine[chip] = wbuf[:, right_rows(chip, core), :]
    gbuf[0] = dot(qbuf[0], br, 1, 1) - dot(qbuf[1], bi, 1, 1)
    gbuf[1] = dot(qbuf[1], br, 1, 1) + dot(qbuf[0], bi, 1, 1)
    for d in range(cols):
        left_outs[d][...] = gbuf[:, left_rows(d), :].astype(left_outs[d].dtype)


def stage(left_parts, q_own, q_other, rec):
    cols = len(left_parts)
    two, wide, rows = left_parts[0].shape
    shots = q_own.shape[3]
    rank = wide * cols
    part = jax.ShapeDtypeStruct((two, wide, rows), F32)
    sent = jax.ShapeDtypeStruct((two, wide, rows), BF)
    outs = [jax.ShapeDtypeStruct(q_own.shape, BF), jax.ShapeDtypeStruct(q_own.shape, F32), part]
    outs += [sent] * (cols - 1)
    scratch = [
        pltpu.VMEM((two, rank, rows), BF),
        pltpu.VMEM((two, rank, shots), BF),
        pltpu.VMEM((two, rank, shots), F32),
        pltpu.VMEM((two, rank, rows), F32),
    ]
    call = on_chip(functools.partial(stage_kernel, cols), outs, scratch, 24 * rank * rows * shots)
    theirs, mine, *terms = call(*left_parts, q_own, q_other, rec)
    return theirs, mine, terms


def picks(near):
    shots = near.shape[1]
    at = lax.broadcasted_iota(jnp.int32, (2 * shots, shots), 0)
    return (at == near).astype(BF)


def mixed(own, nxt, pick, table):
    shots = pick.shape[1]
    part = [dot(own[z], pick[:shots], 1, 0) + dot(nxt[z], pick[shots:], 1, 0) for z in range(2)]
    own = [own[z].astype(F32) for z in range(2)]
    cos, sin, cosp, sinp = table[0:1], table[1:2], table[4:5], table[5:6]
    real = cos * own[0] + sin * own[1] + cosp * part[0] + sinp * part[1]
    imag = cos * own[1] - sin * own[0] + cosp * part[1] - sinp * part[0]
    return real.astype(BF), imag.astype(BF)


def stepped(right, before, here, pick_before, pick_here, cos, sin, eta):
    shots = pick_here.shape[1]
    s = [
        here[z].astype(F32)
        + dot(before[z], pick_before[shots:], 1, 1)
        + dot(here[z], pick_here[:shots], 1, 1)
        for z in range(2)
    ]
    grad = cos * s[0] - sin * s[1], cos * s[1] + sin * s[0]
    return [(right[z].astype(F32) - eta * grad[z]).astype(BF) for z in range(2)]


def table_kernel(rows, table):
    table[...] = rows[...]


def first_kernel(right, right_next, near, table, q):
    q[0], q[1] = mixed(right, right_next, picks(near[1:2]), table)


def middle_kernel(eta, right, right_next, w_prev, w_own, w_next, near, table, q, new):
    prev, own, nxt = picks(near[0:1]), picks(near[1:2]), picks(near[2:3])
    here = stepped(right, w_prev, w_own, prev, own, table[0:1], table[1:2], eta)
    there = stepped(right_next, w_own, w_next, own, nxt, table[2:3], table[3:4], eta)
    new[0], new[1] = here
    q[0], q[1] = mixed(here, there, own, table)


def last_kernel(eta_left, eta_right, right, w_prev, w_own, near, table, left, *refs):
    *terms, new_left, new_right = refs
    prev, own = picks(near[0:1]), picks(near[1:2])
    here = stepped(right, w_prev, w_own, prev, own, table[0:1], table[1:2], eta_right)
    new_right[0], new_right[1] = here
    grad = sum(t[...].astype(F32) for t in terms)
    new_left[...] = (left[...].astype(F32) - eta_left * grad).astype(BF)


def on_device(left_factor, right_factor, recorded, partner, delay):
    shots_dev = recorded.shape[2]
    rows_dev = recorded.shape[1]
    shots_all = partner.shape[0]
    rows_all = rows_dev * lax.axis_size("row")
    blocks = lax.axis_size("col")
    rank_full = left_factor.shape[1] * blocks
    eta_left = 0.1 * math.sqrt(rank_full / shots_all)
    eta_right = 0.05 / math.sqrt(rank_full * rows_all)
    block = lax.axis_index("col")

    def of_block(vector, by):
        return lax.dynamic_slice_in_dim(vector, jnp.mod(block + by, blocks) * shots_dev, shots_dev, 0)

    def near_of(by):
        start = jnp.mod(block + by, blocks) * shots_dev
        return jnp.mod(of_block(partner, by) - start, shots_all)

    near = jnp.stack([near_of(-1), near_of(0), near_of(1)])
    delays = jnp.concatenate([of_block(delay, 0), of_block(delay, 1)]).astype(F32)
    delay_part = dot(delays.astype(BF), picks(near[1:2]), 0, 0)
    theta = 2.0 * math.pi * jnp.stack([delays[:shots_dev], delays[shots_dev:], delay_part]) / NDELAY
    table = jnp.stack([jnp.cos(theta), jnp.sin(theta)], axis=1).reshape(6, shots_dev)
    table = on_chip(table_kernel, jax.ShapeDtypeStruct(table.shape, F32), cost=1 << 30)(table)

    def over_row(q, parts):
        half = lax.all_gather(q, "row", axis=0, axis_index_groups=same_core())
        half, parts = lax.optimization_barrier((half, parts))
        return half, exchanged(half, "row", 1), parts

    shard = jax.ShapeDtypeStruct(right_factor.shape, BF)
    chip = lax.axis_index("row") >> 1
    left, right = left_factor, right_factor
    right_next = passed_along(right, "col", -1)
    parts, right_next = gathered_left(left, right_next, False)
    q = on_chip(first_kernel, shard)(right, right_next, near, table)
    for step in range(ITERS):
        q_own, q_other, parts = over_row(q, parts)
        theirs, mine, terms = stage(parts, q_own, q_other, recorded)
        pair = (mine + exchanged(theirs, "row", 1).astype(F32)).astype(BF)
        total = lax.dynamic_index_in_dim(pair, chip, 0, False).astype(F32)
        for d in range(1, pair.shape[0]):
            sent = lax.dynamic_index_in_dim(pair, chip ^ d, 0, False)
            total = total + exchanged(sent, "row", 2 * d).astype(F32)
        w_own = total.astype(BF)
        terms = [terms[0]] + [exchanged(terms[d], "col", d) for d in range(1, blocks)]
        if step + 1 < ITERS:
            beside = [passed_along(w_own, "col", by) for by in (1, -1)]
            terms, w_own = lax.optimization_barrier((terms, w_own))
            left = (left.astype(F32) - eta_left * sum(t.astype(F32) for t in terms)).astype(BF)
            parts, (w_prev, w_next) = gathered_left(left, beside, True)
            middle = on_chip(functools.partial(middle_kernel, eta_right), [shard, shard])
            q, right = middle(right, right_next, w_prev, w_own, w_next, near, table)
    w_prev = passed_along(w_own, "col", 1)
    outs = [jax.ShapeDtypeStruct(left.shape, BF), shard]
    final = on_chip(functools.partial(last_kernel, eta_left, eta_right), outs)
    return tuple(final(right, w_prev, w_own, near, table, left, *terms))


def solution(mesh):
    in_specs = (P(None, "col", "row"), P(None, "row", "col"), P(None, "row", "col"), P(), P())
    out_specs = (P(None, "col", "row"), P(None, "row", "col"))
    return jax.shard_map(
        on_device, mesh=mesh, in_specs=in_specs, out_specs=out_specs, check_vma=False
    )
```

```python
import functools
import math

import jax
import jax.numpy as jnp
from jax import lax
from jax.experimental import pallas as pl
from jax.experimental.pallas import tpu as pltpu
from jax.sharding import PartitionSpec as P

ITERS = 2
NDELAY = 64
BF = jnp.bfloat16
F32 = jnp.float32


def exchanged(shard, axis, flip):
    size = lax.axis_size(axis)
    return lax.ppermute(shard, axis, [(i, i ^ flip) for i in range(size)])


def passed_along(shard, axis, by):
    size = lax.axis_size(axis)
    return lax.ppermute(shard, axis, [(i, (i + by) % size) for i in range(size)])


def same_core():
    size = lax.axis_size("row")
    return [list(range(core, size, 2)) for core in range(2)]


def gathered_left(shard, small, near_waits):
    size = lax.axis_size("col")
    held, small = lax.optimization_barrier((shard, small))
    parts = [shard]
    for d in range(1, size):
        parts.append(exchanged(held if (d == 1) == near_waits else shard, "col", d))
    return parts, small


def on_chip(kernel, outs, scratch=(), cost=1 << 20):
    return pl.pallas_call(
        kernel,
        out_shape=outs,
        scratch_shapes=list(scratch),
        cost_estimate=pl.CostEstimate(flops=cost, bytes_accessed=1 << 20, transcendentals=0),
        compiler_params=pltpu.CompilerParams(vmem_limit_bytes=48 * 1024 * 1024),
    )


def dot(a, b, ca, cb):
    return lax.dot_general(a, b, (((ca,), (cb,)), ((), ())), preferred_element_type=F32)


def stage_kernel(cols, *refs):
    left_refs, refs = refs[:cols], refs[cols:]
    q_own, q_other, rec, theirs, mine, *refs = refs
    left_outs, (lbuf, qbuf, wbuf, gbuf) = refs[:cols], refs[cols:]
    me, core = lax.axis_index("col"), lax.axis_index("row") & 1
    wide, narrow, chips = left_refs[0].shape[1], q_own.shape[2], q_own.shape[0]

    def left_rows(d):
        return pl.ds(pl.multiple_of((me ^ d) * wide, wide), wide)

    def right_rows(chip, which):
        return pl.ds(pl.multiple_of((2 * chip + which) * narrow, narrow), narrow)

    for d in range(cols):
        lbuf[:, left_rows(d), :] = left_refs[d][...]
    for chip in range(chips):
        qbuf[:, right_rows(chip, core), :] = q_own[chip]
        qbuf[:, right_rows(chip, core ^ 1), :] = q_other[chip]
    br = dot(lbuf[0], qbuf[0], 0, 0) + dot(lbuf[1], qbuf[1], 0, 0) - rec[0].astype(F32)
    bi = dot(lbuf[1], qbuf[0], 0, 0) - dot(lbuf[0], qbuf[1], 0, 0) - rec[1].astype(F32)
    br, bi = br.astype(BF), bi.astype(BF)
    wbuf[0] = dot(lbuf[0], br, 1, 0) + dot(lbuf[1], bi, 1, 0)
    wbuf[1] = dot(lbuf[1], br, 1, 0) - dot(lbuf[0], bi, 1, 0)
    for chip in range(chips):
        theirs[chip] = wbuf[:, right_rows(chip, core ^ 1), :].astype(BF)
        mine[chip] = wbuf[:, right_rows(chip, core), :]
    gbuf[0] = dot(qbuf[0], br, 1, 1) - dot(qbuf[1], bi, 1, 1)
    gbuf[1] = dot(qbuf[1], br, 1, 1) + dot(qbuf[0], bi, 1, 1)
    for d in range(cols):
        left_outs[d][...] = gbuf[:, left_rows(d), :].astype(left_outs[d].dtype)


def stage(left_parts, q_own, q_other, rec):
    cols = len(left_parts)
    two, wide, rows = left_parts[0].shape
    shots = q_own.shape[3]
    rank = wide * cols
    part = jax.ShapeDtypeStruct((two, wide, rows), F32)
    sent = jax.ShapeDtypeStruct((two, wide, rows), BF)
    outs = [jax.ShapeDtypeStruct(q_own.shape, BF), jax.ShapeDtypeStruct(q_own.shape, F32), part]
    outs += [sent] * (cols - 1)
    scratch = [
        pltpu.VMEM((two, rank, rows), BF),
        pltpu.VMEM((two, rank, shots), BF),
        pltpu.VMEM((two, rank, shots), F32),
        pltpu.VMEM((two, rank, rows), F32),
    ]
    call = on_chip(functools.partial(stage_kernel, cols), outs, scratch, 24 * rank * rows * shots)
    theirs, mine, *terms = call(*left_parts, q_own, q_other, rec)
    return theirs, mine, terms


def picks(near):
    shots = near.shape[1]
    at = lax.broadcasted_iota(jnp.int32, (2 * shots, shots), 0)
    return (at == near).astype(BF)


def stacked(x):
    return x[...].reshape(-1, x.shape[2])


def mixed(own, nxt, pick, table):
    shots = pick.shape[1]
    half = own.shape[0] // 2
    part = dot(own, pick[:shots], 1, 0) + dot(nxt, pick[shots:], 1, 0)
    own = own.astype(F32)
    cos, sin, cosp, sinp = table[0:1], table[1:2], table[4:5], table[5:6]
    real = cos * own[:half] + sin * own[half:] + cosp * part[:half] + sinp * part[half:]
    imag = cos * own[half:] - sin * own[:half] + cosp * part[half:] - sinp * part[:half]
    return jnp.concatenate([real, imag]).astype(BF)


def stepped(right, before, here, pick_before, pick_here, cos, sin, eta):
    shots = pick_here.shape[1]
    half = here.shape[0] // 2
    s = here.astype(F32) + dot(before, pick_before[shots:], 1, 1) + dot(here, pick_here[:shots], 1, 1)
    grad = jnp.concatenate([cos * s[:half] - sin * s[half:], cos * s[half:] + sin * s[:half]])
    return (right.astype(F32) - eta * grad).astype(BF)


def table_kernel(rows, table):
    table[...] = rows[...]


def first_kernel(right, right_next, near, table, q):
    q[...] = mixed(stacked(right), stacked(right_next), picks(near[1:2]), table).reshape(q.shape)


def middle_kernel(eta, right, right_next, w_prev, w_own, w_next, near, table, q, new):
    prev, own, nxt = picks(near[0:1]), picks(near[1:2]), picks(near[2:3])
    w_prev, w_own, w_next = stacked(w_prev), stacked(w_own), stacked(w_next)
    here = stepped(stacked(right), w_prev, w_own, prev, own, table[0:1], table[1:2], eta)
    there = stepped(stacked(right_next), w_own, w_next, own, nxt, table[2:3], table[3:4], eta)
    new[...] = here.reshape(new.shape)
    q[...] = mixed(here, there, own, table).reshape(q.shape)


def last_kernel(eta_left, eta_right, right, w_prev, w_own, near, table, left, *refs):
    *terms, new_left, new_right = refs
    prev, own = picks(near[0:1]), picks(near[1:2])
    here = stepped(
        stacked(right), stacked(w_prev), stacked(w_own), prev, own, table[0:1], table[1:2], eta_right
    )
    new_right[...] = here.reshape(new_right.shape)
    grad = sum(t[...].astype(F32) for t in terms)
    new_left[...] = (left[...].astype(F32) - eta_left * grad).astype(BF)


def on_device(left_factor, right_factor, recorded, partner, delay):
    shots_dev = recorded.shape[2]
    rows_dev = recorded.shape[1]
    shots_all = partner.shape[0]
    rows_all = rows_dev * lax.axis_size("row")
    blocks = lax.axis_size("col")
    rank_full = left_factor.shape[1] * blocks
    eta_left = 0.1 * math.sqrt(rank_full / shots_all)
    eta_right = 0.05 / math.sqrt(rank_full * rows_all)
    block = lax.axis_index("col")

    def of_block(vector, by):
        return lax.dynamic_slice_in_dim(vector, jnp.mod(block + by, blocks) * shots_dev, shots_dev, 0)

    def near_of(by):
        start = jnp.mod(block + by, blocks) * shots_dev
        return jnp.mod(of_block(partner, by) - start, shots_all)

    near = jnp.stack([near_of(-1), near_of(0), near_of(1)])
    delays = jnp.concatenate([of_block(delay, 0), of_block(delay, 1)]).astype(F32)
    delay_part = dot(delays.astype(BF), picks(near[1:2]), 0, 0)
    theta = 2.0 * math.pi * jnp.stack([delays[:shots_dev], delays[shots_dev:], delay_part]) / NDELAY
    table = jnp.stack([jnp.cos(theta), jnp.sin(theta)], axis=1).reshape(6, shots_dev)
    table = on_chip(table_kernel, jax.ShapeDtypeStruct(table.shape, F32), cost=1 << 30)(table)

    def over_row(q, parts):
        half = lax.all_gather(q, "row", axis=0, axis_index_groups=same_core())
        half, parts = lax.optimization_barrier((half, parts))
        return half, exchanged(half, "row", 1), parts

    shard = jax.ShapeDtypeStruct(right_factor.shape, BF)
    chip = lax.axis_index("row") >> 1
    left, right = left_factor, right_factor
    right_next = passed_along(right, "col", -1)
    parts, right_next = gathered_left(left, right_next, False)
    q = on_chip(first_kernel, shard)(right, right_next, near, table)
    for step in range(ITERS):
        q_own, q_other, parts = over_row(q, parts)
        theirs, mine, terms = stage(parts, q_own, q_other, recorded)
        pair = (mine + exchanged(theirs, "row", 1).astype(F32)).astype(BF)
        sums = [lax.dynamic_index_in_dim(pair, chip, 0, False)]
        for d in range(1, pair.shape[0]):
            sent = lax.dynamic_index_in_dim(pair, chip ^ d, 0, False)
            sums.append(exchanged(sent, "row", 2 * d))
        terms = [terms[0]] + [exchanged(terms[d], "col", d) for d in range(1, blocks)]
        early = slice(2, 3) if step + 1 < ITERS else slice(1, 3)
        sums, terms[early] = lax.optimization_barrier((sums, terms[early]))
        w_own = sum(part.astype(F32) for part in sums).astype(BF)
        if step + 1 < ITERS:
            beside = [passed_along(w_own, "col", by) for by in (1, -1)]
            terms, w_own = lax.optimization_barrier((terms, w_own))
            left = (left.astype(F32) - eta_left * sum(t.astype(F32) for t in terms)).astype(BF)
            parts, (w_prev, w_next) = gathered_left(left, beside, True)
            middle = on_chip(functools.partial(middle_kernel, eta_right), [shard, shard])
            q, right = middle(right, right_next, w_prev, w_own, w_next, near, table)
    w_prev = passed_along(w_own, "col", 1)
    outs = [jax.ShapeDtypeStruct(left.shape, BF), shard]
    final = on_chip(functools.partial(last_kernel, eta_left, eta_right), outs)
    return tuple(final(right, w_prev, w_own, near, table, left, *terms))


def solution(mesh):
    in_specs = (P(None, "col", "row"), P(None, "row", "col"), P(None, "row", "col"), P(), P())
    out_specs = (P(None, "col", "row"), P(None, "row", "col"))
    return jax.shard_map(
        on_device, mesh=mesh, in_specs=in_specs, out_specs=out_specs, check_vma=False
    )
```

```python
import functools
import math

import jax
import jax.numpy as jnp
from jax import lax
from jax.experimental import pallas as pl
from jax.experimental.pallas import tpu as pltpu
from jax.sharding import PartitionSpec as P

ITERS = 2
NDELAY = 64
BF = jnp.bfloat16
F32 = jnp.float32


def exchanged(shard, axis, flip):
    size = lax.axis_size(axis)
    return lax.ppermute(shard, axis, [(i, i ^ flip) for i in range(size)])


def passed_along(shard, axis, by):
    size = lax.axis_size(axis)
    return lax.ppermute(shard, axis, [(i, (i + by) % size) for i in range(size)])


def gathered_left(shard, small, near_waits):
    size = lax.axis_size("col")
    held, small = lax.optimization_barrier((shard, small))
    parts = [shard]
    for d in range(1, size):
        parts.append(exchanged(held if (d == 1) == near_waits else shard, "col", d))
    return parts, small


def on_chip(kernel, outs, scratch=(), cost=1 << 20):
    return pl.pallas_call(
        kernel,
        out_shape=outs,
        scratch_shapes=list(scratch),
        cost_estimate=pl.CostEstimate(flops=cost, bytes_accessed=1 << 20, transcendentals=0),
        compiler_params=pltpu.CompilerParams(vmem_limit_bytes=48 * 1024 * 1024),
    )


def dot(a, b, ca, cb):
    return lax.dot_general(a, b, (((ca,), (cb,)), ((), ())), preferred_element_type=F32)


def stage_kernel(cols, *refs):
    left_refs, refs = refs[:cols], refs[cols:]
    q, rec, theirs, mine, *refs = refs
    left_outs, (lbuf, qbuf, wbuf, gbuf) = refs[:cols], refs[cols:]
    me, core = lax.axis_index("col"), lax.axis_index("row") & 1
    wide, narrow, chips = left_refs[0].shape[1], q.shape[2], q.shape[0] // 2

    def left_rows(d):
        return pl.ds(pl.multiple_of((me ^ d) * wide, wide), wide)

    def right_rows(chip, which):
        return pl.ds(pl.multiple_of((2 * chip + which) * narrow, narrow), narrow)

    for d in range(cols):
        lbuf[:, left_rows(d), :] = left_refs[d][...]
    for device in range(2 * chips):
        qbuf[:, device * narrow : (device + 1) * narrow, :] = q[device]
    br = dot(lbuf[0], qbuf[0], 0, 0) + dot(lbuf[1], qbuf[1], 0, 0) - rec[0].astype(F32)
    bi = dot(lbuf[1], qbuf[0], 0, 0) - dot(lbuf[0], qbuf[1], 0, 0) - rec[1].astype(F32)
    br, bi = br.astype(BF), bi.astype(BF)
    wbuf[0] = dot(lbuf[0], br, 1, 0) + dot(lbuf[1], bi, 1, 0)
    wbuf[1] = dot(lbuf[1], br, 1, 0) - dot(lbuf[0], bi, 1, 0)
    for chip in range(chips):
        theirs[chip] = wbuf[:, right_rows(chip, core ^ 1), :].astype(BF)
        mine[chip] = wbuf[:, right_rows(chip, core), :]
    gbuf[0] = dot(qbuf[0], br, 1, 1) - dot(qbuf[1], bi, 1, 1)
    gbuf[1] = dot(qbuf[1], br, 1, 1) + dot(qbuf[0], bi, 1, 1)
    for d in range(cols):
        left_outs[d][...] = gbuf[:, left_rows(d), :].astype(left_outs[d].dtype)


def stage(left_parts, q, rec):
    cols = len(left_parts)
    two, wide, rows = left_parts[0].shape
    devices, two, narrow, shots = q.shape
    rank = wide * cols
    part = jax.ShapeDtypeStruct((two, wide, rows), F32)
    sent = jax.ShapeDtypeStruct((two, wide, rows), BF)
    halves = (devices // 2, two, narrow, shots)
    outs = [jax.ShapeDtypeStruct(halves, BF), jax.ShapeDtypeStruct(halves, F32), part]
    outs += [sent] * (cols - 1)
    scratch = [
        pltpu.VMEM((two, rank, rows), BF),
        pltpu.VMEM((two, rank, shots), BF),
        pltpu.VMEM((two, rank, shots), F32),
        pltpu.VMEM((two, rank, rows), F32),
    ]
    call = on_chip(functools.partial(stage_kernel, cols), outs, scratch, 24 * rank * rows * shots)
    theirs, mine, *terms = call(*left_parts, q, rec)
    return theirs, mine, terms


def picks(near):
    shots = near.shape[1]
    at = lax.broadcasted_iota(jnp.int32, (2 * shots, shots), 0)
    return (at == near).astype(BF)


def stacked(x):
    return x[...].reshape(-1, x.shape[2])


def mixed(own, nxt, pick, table):
    shots = pick.shape[1]
    half = own.shape[0] // 2
    part = dot(own, pick[:shots], 1, 0) + dot(nxt, pick[shots:], 1, 0)
    own = own.astype(F32)
    cos, sin, cosp, sinp = table[0:1], table[1:2], table[4:5], table[5:6]
    real = cos * own[:half] + sin * own[half:] + cosp * part[:half] + sinp * part[half:]
    imag = cos * own[half:] - sin * own[:half] + cosp * part[half:] - sinp * part[:half]
    return jnp.concatenate([real, imag]).astype(BF)


def stepped(right, before, here, pick_before, pick_here, cos, sin, eta):
    shots = pick_here.shape[1]
    half = here.shape[0] // 2
    s = here.astype(F32) + dot(before, pick_before[shots:], 1, 1) + dot(here, pick_here[:shots], 1, 1)
    grad = jnp.concatenate([cos * s[:half] - sin * s[half:], cos * s[half:] + sin * s[:half]])
    return (right.astype(F32) - eta * grad).astype(BF)


def table_kernel(rows, table):
    table[...] = rows[...]


def first_kernel(right, right_next, near, table, q):
    q[...] = mixed(stacked(right), stacked(right_next), picks(near[1:2]), table).reshape(q.shape)


def middle_kernel(eta, right, right_next, w_prev, w_own, w_next, near, table, q, new):
    prev, own, nxt = picks(near[0:1]), picks(near[1:2]), picks(near[2:3])
    w_prev, w_own, w_next = stacked(w_prev), stacked(w_own), stacked(w_next)
    here = stepped(stacked(right), w_prev, w_own, prev, own, table[0:1], table[1:2], eta)
    there = stepped(stacked(right_next), w_own, w_next, own, nxt, table[2:3], table[3:4], eta)
    new[...] = here.reshape(new.shape)
    q[...] = mixed(here, there, own, table).reshape(q.shape)


def last_kernel(eta_left, eta_right, right, w_prev, w_own, near, table, left, *refs):
    *terms, new_left, new_right = refs
    prev, own = picks(near[0:1]), picks(near[1:2])
    here = stepped(
        stacked(right), stacked(w_prev), stacked(w_own), prev, own, table[0:1], table[1:2], eta_right
    )
    new_right[...] = here.reshape(new_right.shape)
    grad = sum(t[...].astype(F32) for t in terms)
    new_left[...] = (left[...].astype(F32) - eta_left * grad).astype(BF)


def on_device(left_factor, right_factor, recorded, partner, delay):
    shots_dev = recorded.shape[2]
    rows_dev = recorded.shape[1]
    shots_all = partner.shape[0]
    rows_all = rows_dev * lax.axis_size("row")
    blocks = lax.axis_size("col")
    rank_full = left_factor.shape[1] * blocks
    eta_left = 0.1 * math.sqrt(rank_full / shots_all)
    eta_right = 0.05 / math.sqrt(rank_full * rows_all)
    block = lax.axis_index("col")

    def of_block(vector, by):
        return lax.dynamic_slice_in_dim(vector, jnp.mod(block + by, blocks) * shots_dev, shots_dev, 0)

    def near_of(by):
        start = jnp.mod(block + by, blocks) * shots_dev
        return jnp.mod(of_block(partner, by) - start, shots_all)

    near = jnp.stack([near_of(-1), near_of(0), near_of(1)])
    delays = jnp.concatenate([of_block(delay, 0), of_block(delay, 1)]).astype(F32)
    delay_part = dot(delays.astype(BF), picks(near[1:2]), 0, 0)
    theta = 2.0 * math.pi * jnp.stack([delays[:shots_dev], delays[shots_dev:], delay_part]) / NDELAY
    table = jnp.stack([jnp.cos(theta), jnp.sin(theta)], axis=1).reshape(6, shots_dev)
    table = on_chip(table_kernel, jax.ShapeDtypeStruct(table.shape, F32), cost=1 << 30)(table)

    shard = jax.ShapeDtypeStruct(right_factor.shape, BF)
    chip = lax.axis_index("row") >> 1
    left, right = left_factor, right_factor
    right_next = passed_along(right, "col", -1)
    parts, right_next = gathered_left(left, right_next, False)
    q = on_chip(first_kernel, shard)(right, right_next, near, table)
    for step in range(ITERS):
        q = lax.all_gather(q, "row", axis=0)
        q, parts = lax.optimization_barrier((q, parts))
        theirs, mine, terms = stage(parts, q, recorded)
        pair = (mine + exchanged(theirs, "row", 1).astype(F32)).astype(BF)
        sums = [lax.dynamic_index_in_dim(pair, chip, 0, False)]
        for d in range(1, pair.shape[0]):
            sent = lax.dynamic_index_in_dim(pair, chip ^ d, 0, False)
            sums.append(exchanged(sent, "row", 2 * d))
        terms = [terms[0]] + [exchanged(terms[d], "col", d) for d in range(1, blocks)]
        early = [d for d in ((1, 3) if step + 1 < ITERS else (1, 2)) if d < blocks]
        sums, held = lax.optimization_barrier((sums, [terms[d] for d in early]))
        for d, term in zip(early, held):
            terms[d] = term
        w_own = sum(part.astype(F32) for part in sums).astype(BF)
        if step + 1 < ITERS:
            beside = [passed_along(w_own, "col", by) for by in (1, -1)]
            terms, w_own = lax.optimization_barrier((terms, w_own))
            left = (left.astype(F32) - eta_left * sum(t.astype(F32) for t in terms)).astype(BF)
            parts, (w_prev, w_next) = gathered_left(left, beside, True)
            middle = on_chip(functools.partial(middle_kernel, eta_right), [shard, shard])
            q, right = middle(right, right_next, w_prev, w_own, w_next, near, table)
    w_prev = passed_along(w_own, "col", 1)
    outs = [jax.ShapeDtypeStruct(left.shape, BF), shard]
    final = on_chip(functools.partial(last_kernel, eta_left, eta_right), outs)
    return tuple(final(right, w_prev, w_own, near, table, left, *terms))


def solution(mesh):
    in_specs = (P(None, "col", "row"), P(None, "row", "col"), P(None, "row", "col"), P(), P())
    out_specs = (P(None, "col", "row"), P(None, "row", "col"))
    return jax.shard_map(
        on_device, mesh=mesh, in_specs=in_specs, out_specs=out_specs, check_vma=False
    )
```
